32 devices in a mesh: scen: 2 (over x), tile: 16 (over z, y, core).
Axes of the slice: x: 2, y: 2, z: 4, core: 2. Of those that a mesh axis runs over, the one named last changes fastest.
Arguments:
- regional: float32 [4096, 768], P(('scen', 'tile')), parts along dimension 0, may hold values from -6 to 6
- row_weight: float32 [4096, 1], P(('scen', 'tile')), parts along dimension 0, may hold values from 0.25 to 1.75
- row_seg: int32 [4096, 1], P(('scen', 'tile')), parts along dimension 0, may hold values from 0 to 15; in each aligned block of 128 rows (0 to 127, 128 to 255, ...) at most 16 rows name the same one
- row_col: int32 [4096, 1], P(('scen', 'tile')), parts along dimension 0, may hold values from 0 to 63
- box_owner: int32 [8], P('scen'), parts along dimension 0, may hold values from 0 to 3, as said below
- cell_class: int32 [512, 128, 128], P(('scen', 'tile')), parts along dimension 0, may hold values from 0 to 31
- soil_props: float32 [3, 16], replicated, may hold values from 0.5 to 2
- build_props: float32 [16, 3, 16], replicated, may hold values from 0.5 to 2
- real_ids: int32 [2], P('scen'), parts along dimension 0, may hold values from 0 to 15
- disp_prev: float32 [512, 1, 3, 128, 128], P(('scen', 'tile')), parts along dimension 0, may hold values from -6 to 6
- disp_now: float32 [512, 1, 3, 128, 128], P(('scen', 'tile')), parts along dimension 0, may hold values from -6 to 6
Outputs:
- disp_next: float32 [512, 1, 3, 128, 128], P(('scen', 'tile')), parts along dimension 0
The draws below stay inside these ranges and needn't reach their ends.
There are 2 independent parts, one for each index of `scen`. The reference program is written for one: setup_inputs(seed, part) draws one part's arguments, and reference() takes and returns one part's arrays. A program takes and returns all parts, laid end to end along the dimension named above; an argument that names none is the same for every part. Nothing has to cross between parts.
Inputs may be any that keep to these rules, and one draw needn't show every extreme that they name: `row_seg`: the rows of one device name one segment at most 16 times; some device's rows name some segment exactly 16 times. `box_owner`: each owner slot holds exactly one box. `cell_class`: classes below 16 are soil, the others building.
All inputs are finite; a program needn't handle non-finite values.
Results may differ from the reference program's by a relative error of at most 0.00005.
Values sent between devices are 32-bit elements; how exact they have to be, the bound alone decides.
A program may use at most 128 MiB of HBM per device.

```python
import math
import jax
import jax.numpy as jnp
import numpy as np
from jax import lax

XS = 16
Y = 128
Z = 128
ROWS_DEV = 128
REALS = 1
CLASSES = 16
TABLE = 16
SPAN = 4
BOXES = 4
CAP = 16
ROWS = 2048
SEGX = 256
N_TILE = 16


def draw_box_owner(key, part):
    return jax.random.permutation(jax.random.fold_in(key, 7331), BOXES).astype(jnp.int32)


def place_ends(values, own_key, least, top_value):
    longest = values.shape.index(max(values.shape))
    spots = []
    for shift in (0, 1):
        where = [jax.random.randint(jax.random.fold_in(own_key, axis), (), 0, length) for axis, length in enumerate(values.shape)]
        where[longest] = (where[longest] + shift) % values.shape[longest]
        spots.append(tuple(where))
    return values.at[spots[0]].set(least).at[spots[1]].set(top_value)


def block_levels(key, extent, pieces, least, largest):
    loudness, own = 1.0, jax.random.fold_in(key, 6)
    for axis_at, shards_of in pieces:
        heights = jnp.exp(jax.random.uniform(jax.random.fold_in(own, axis_at), (shards_of,), jnp.float32, least / len(pieces), largest / len(pieces)))
        loudness = loudness * jnp.repeat(heights, extent[axis_at] // shards_of).reshape([-1 if axis == axis_at else 1 for axis in range(len(extent))])
    return loudness


def routed_block(stream_key, own, number, rows, count, top, limit, skew):
    sequence = jax.random.permutation(stream_key, count)
    packed, ordinary = portions_of(count, rows * top, limit, skew, True), portions_of(count, rows * top, limit, skew, False)
    places = jnp.arange(count)

    def named(sizes, offset_by):
        used = int((sizes > 0).sum())
        fixed = max(1, used // 4)
        shifted = fixed + (places - fixed + offset_by * (used - fixed)) % max(1, count - fixed)
        return jnp.zeros((count,), jnp.int32).at[sequence[jnp.where(places < fixed, places, shifted)]].set(jnp.asarray(sizes, jnp.int32))

    sizes = jnp.where(number % 4 == 0, named(packed, number // 4), named(ordinary, number - number // 4 - 1))
    mixed = jax.random.permutation(jax.random.fold_in(own, 3), count)
    source_of, taker = mixed[0:count // 2 * 2:2], mixed[1:count // 2 * 2:2]
    margin = jnp.minimum(sizes[source_of] - 1, limit - sizes[taker]) // 2
    margin = jnp.where((source_of == sequence[0]) | (taker == sequence[0]) | (sizes[taker] == 0), 0, jnp.maximum(margin, 0))
    shifted = jax.random.randint(jax.random.fold_in(own, 4), (count // 2,), 0, 1 << 20) % (margin + 1)
    sizes = sizes.at[source_of].add(-shifted).at[taker].add(shifted)
    items = jnp.searchsorted(jnp.cumsum(sizes), jnp.arange(rows * top), side="right").astype(jnp.int32)
    table = items.reshape(top, rows).T
    table = table[jax.random.permutation(jax.random.fold_in(own, 1), rows)]
    offset_by = jax.random.randint(jax.random.fold_in(own, 2), (rows, 1), 0, top)
    return jnp.take_along_axis(table, (jnp.arange(top)[None, :] + offset_by) % top, axis=1)


def portions_of(number_of, total, reach, lean, full):
    loads = [(1 << 20) // math.isqrt(grade ** lean) + 1 for grade in range(1, number_of + 1)]
    largest = reach if full else min(reach, max(-(-total // number_of), total * loads[0] // sum(loads)))
    least = 1 if total - largest >= number_of - 1 else 0
    holding, rest = [largest] + [least] * (number_of - 1), total - largest - least * (number_of - 1)
    while rest > 0:
        free = [i for i in range(1, number_of) if holding[i] < largest] or [i for i in range(1, number_of) if holding[i] < reach]
        mass, budget = sum([loads[i] for i in free]), rest
        for i in free:
            more = min(reach - holding[i], max(1, budget * loads[i] // mass), rest)
            holding[i] = holding[i] + more
            rest = rest - more
    return np.array(holding)


def scatter_about(stream_key, extent, scale, bound, split=(), kind=jnp.bfloat16):
    values = jax.random.normal(stream_key, extent, jnp.float32) * scale
    if len(split) > 0:
        values = block_levels(stream_key, extent, split, -0.22, 0.18) * values
    return jnp.clip(values, min=-bound, max=bound).astype(kind)


def setup_inputs(seed: int = 0, part: int = 0) -> dict:
    splits = jax.random.split(jax.random.key(seed), 12)
    part_keys = jax.random.split(jax.random.fold_in(splits[11], part), 12)
    regional = scatter_about(part_keys[0], (ROWS, 6 * Z), 1.0, 6.0, ((0, 16),), jnp.float32)
    row_weight = jnp.clip(0.25 + 1.5 * jax.random.uniform(part_keys[1], (ROWS, 1), jnp.float32) ** block_levels(part_keys[1], (ROWS, 1), ((0, 16),), -0.2, 0.2), 0.25, 1.75)
    row_seg_keys = jax.random.split(jax.random.fold_in(part_keys[2], 1), ROWS // ROWS_DEV)
    row_seg_turns = jax.random.permutation(jax.random.fold_in(part_keys[2], 3), ROWS // ROWS_DEV)
    row_seg = jax.vmap(lambda own, number: routed_block(jax.random.fold_in(part_keys[2], 2), own, number, ROWS_DEV, BOXES * SPAN, 1, CAP, 2))(row_seg_keys, row_seg_turns).reshape((ROWS, 1))
    row_col = place_ends(jax.random.randint(part_keys[3], (ROWS, 1), 0, 4 * XS), jax.random.fold_in(part_keys[3], 1), 0, (4 * XS) - 1).astype(jnp.int32)
    box_owner = draw_box_owner(jax.random.fold_in(jax.random.fold_in(splits[11], part), 71), part)
    cell_class = place_ends(jax.random.randint(part_keys[5], (SEGX, Y, Z), 0, 2 * CLASSES), jax.random.fold_in(part_keys[5], 1), 0, (2 * CLASSES) - 1).astype(jnp.int32)
    soil_props = jnp.clip(jax.random.uniform(splits[6], (3, CLASSES), jnp.float32, 0.5, 2.0), 0.5, 2.0)
    build_props = jnp.clip(jax.random.uniform(splits[7], (TABLE, 3, CLASSES), jnp.float32, 0.5, 2.0), 0.5, 2.0)
    real_ids = jax.random.randint(part_keys[8], (REALS,), 0, TABLE).astype(jnp.int32)
    disp_prev = scatter_about(part_keys[9], (SEGX, REALS, 3, Y, Z), 1.0, 6.0, ((0, 16),), jnp.float32)
    disp_now = scatter_about(part_keys[10], (SEGX, REALS, 3, Y, Z), 1.0, 6.0, ((0, 16),), jnp.float32)
    return dict(regional=regional, row_weight=row_weight, row_seg=row_seg, row_col=row_col, box_owner=box_owner, cell_class=cell_class, soil_props=soil_props, build_props=build_props, real_ids=real_ids, disp_prev=disp_prev, disp_now=disp_now)


TIME_STEP = 0.04


def window(array, trim, axis, delta):
    index = []
    for dim in range(array.ndim):
        if dim in (0, 3, 4):
            shift = delta if dim == axis else 0
            index.append(slice(trim + shift, array.shape[dim] - trim + shift))
        else:
            index.append(slice(None))
    return array[tuple(index)]


def widen(array, width):
    return jnp.pad(array, ((0, 0), (0, 0), (0, 0), (width, width), (width, width)))


def elastic(disp_ext, bulk_ext, shear_ext):
    disp = widen(disp_ext, 2)
    bulk = widen(bulk_ext, 1)
    shear = widen(shear_ext, 1)
    centre = window(disp, 2, 0, 0)
    shear_mid = window(shear, 1, 0, 0)
    diffusion = None
    for axis in (0, 3, 4):
        upper = window(disp, 2, axis, 1)
        lower = window(disp, 2, axis, -1)
        face_up = 0.5 * (shear_mid + window(shear, 1, axis, 1))
        face_down = 0.5 * (shear_mid + window(shear, 1, axis, -1))
        term = face_up * (upper - centre) - face_down * (centre - lower)
        diffusion = term if diffusion is None else diffusion + term
    spread = None
    for comp, axis in ((0, 0), (1, 3), (2, 4)):
        part = disp[:, :, comp:comp + 1]
        term = 0.5 * (window(part, 1, axis, 1) - window(part, 1, axis, -1))
        spread = term if spread is None else spread + term
    flux = bulk * spread
    pushes = []
    for axis in (0, 3, 4):
        pushes.append(0.5 * (window(flux, 1, axis, 1) - window(flux, 1, axis, -1)))
    return diffusion + jnp.concatenate(pushes, axis=2)


def reference(regional, row_weight, row_seg, row_col, box_owner, cell_class, soil_props, build_props, real_ids, disp_prev, disp_now):
    offset_cells = (SPAN // 2) * XS
    segment = row_seg[:, 0]
    target = box_owner[segment // SPAN] * SPAN + segment % SPAN
    index = (target * (4 * XS) + row_col[:, 0]).astype(jnp.int32)
    band = jnp.zeros((N_TILE * 4 * XS, 6 * Z), jnp.float32).at[index].add(regional * row_weight)
    band = jnp.transpose(band.reshape(BOXES, SPAN * XS, 4, 2, 3, Z), (0, 1, 3, 4, 2, 5))
    soil = jnp.broadcast_to(soil_props[None], (REALS, 3, CLASSES))
    table = jnp.concatenate([soil, build_props[real_ids]], axis=2)
    classes = jnp.roll(cell_class, -offset_cells, axis=0).reshape(BOXES, SPAN * XS, Y, Z)
    before_all = jnp.roll(disp_prev, -offset_cells, axis=0).reshape(BOXES, SPAN * XS, REALS, 3, Y, Z)
    now_all = jnp.roll(disp_now, -offset_cells, axis=0).reshape(BOXES, SPAN * XS, REALS, 3, Y, Z)
    rows_y = jnp.arange(Y, dtype=jnp.int32)
    outer = jnp.logical_or(rows_y < 2, rows_y >= Y - 2).astype(jnp.float32).reshape(1, 1, 1, Y, 1)
    inner = 1.0 - outer
    pad_two = ((2, 2), (0, 0), (0, 0), (0, 0), (0, 0))

    def one_box(items):
        cls, bnd, before, current = items
        values = jnp.transpose(jnp.take(table, cls, axis=2), (2, 0, 1, 3, 4))
        values = jnp.pad(values, ((1, 1), (0, 0), (0, 0), (0, 0), (0, 0)))
        lam_mu = values[:, :, 0:1] + values[:, :, 1:2]
        shear = values[:, :, 1:2]
        inverse = values[1:-1, :, 2:3]
        free = jnp.zeros((SPAN * XS, 2, 3, Y, Z), jnp.float32)
        for place_slot, row in enumerate((1, 2, Y - 3, Y - 2)):
            free = free.at[:, :, :, row].set(bnd[:, :, :, place_slot])
        for level in range(2):
            drive = jnp.pad(free[:, level:level + 1], pad_two)
            from_outer = elastic(drive * outer, lam_mu, shear)
            from_inner = elastic(drive * inner, lam_mu, shear)
            force = inner * from_outer - outer * from_inner
            rhs = elastic(jnp.pad(current, pad_two), lam_mu, shear) + force
            before, current = current, 2.0 * current - before + TIME_STEP * inverse * rhs
        return current

    result = lax.map(one_box, (classes, band, before_all, now_all))
    result = result.reshape(N_TILE * XS, REALS, 3, Y, Z)
    return jnp.roll(result, offset_cells, axis=0)
```

```python
import functools

import jax
import jax.numpy as jnp
from jax import lax
from jax.experimental import pallas as pl
from jax.experimental.pallas import tpu as pltpu
from jax.sharding import PartitionSpec as P

SPAN = 4
TIME_STEP = 0.04
HIGHEST = lax.Precision.HIGHEST
MESH = pl.DeviceIdType.MESH


def above(a, axis):
    size = a.shape[axis]
    at = lax.broadcasted_iota(jnp.int32, a.shape, axis)
    return jnp.where(at == size - 1, 0.0, pltpu.roll(a, size - 1, axis))


def below(a, axis, edge=0.0):
    at = lax.broadcasted_iota(jnp.int32, a.shape, axis)
    return jnp.where(at == 0, edge, pltpu.roll(a, 1, axis))


def volume(xp, xm, vy, vz, bulk):
    total = (xp - xm) + (above(vy, 0) - below(vy, 0)) + (above(vz, 1) - below(vz, 1))
    return bulk * total


def elastic(now, nxt, prv, half, half_nxt, half_prv, g, g_nxt, g_prv):
    face_xp = half + half_nxt
    face_xm = half + half_prv
    face_y = half + above(half, 0)
    face_z = half + above(half, 1)
    push = (
        g_nxt - g_prv,
        above(g, 0) - below(g, 0),
        above(g, 1) - below(g, 1),
    )
    result = []
    for i in range(3):
        v = now[i]
        total = face_xp * (nxt[i] - v) - face_xm * (v - prv[i])
        edge = half * v
        for axis, face in ((0, face_y), (1, face_z)):
            flow = face * (above(v, axis) - v)
            total = total + (flow - below(flow, axis, edge))
        result.append(total + push[i])
    return result


def body(
    count,
    cap,
    regional_ref,
    weight_ref,
    seg_ref,
    col_ref,
    owner_ref,
    table_ref,
    class_ref,
    prev_ref,
    now_ref,
    out_ref,
    cls,
    before,
    d0,
    d1,
    half,
    bulk,
    inv,
    g,
    mat,
    band0,
    band1,
    delta,
    gs,
    send,
    recv,
    local_sem,
    a2a_send,
    a2a_recv,
    halo_send,
    halo_recv,
):
    me = lax.axis_index("tile")
    position = lax.rem(me + count - SPAN // 2, SPAN)
    right = lax.rem(me + 1, count)
    left = lax.rem(me + count - 1, count)
    planes, depth = cls.shape[0], cls.shape[2]
    across = cls.shape[1]
    has_left, has_right = position > 0, position < SPAN - 1

    load_now = pltpu.make_async_copy(now_ref, d0.at[pl.ds(2, planes)], local_sem.at[0])
    load_class = pltpu.make_async_copy(class_ref, cls, local_sem.at[1])
    load_prev = pltpu.make_async_copy(prev_ref, before, local_sem.at[2])
    load_now.start()
    load_class.start()
    load_prev.start()

    barrier = pltpu.get_barrier_semaphore()

    def greet(k, carry):
        pl.semaphore_signal(
            barrier, inc=1, device_id={"tile": lax.rem(me + k, count)}, device_id_type=MESH
        )
        return carry

    lax.fori_loop(1, count, greet, 0)

    rows = regional_ref.shape[0]
    boxes = owner_ref.shape[1]
    seg = seg_ref[...]
    box_ids = lax.broadcasted_iota(jnp.int32, (rows, boxes), 1)
    owner = jnp.sum(
        jnp.where(seg // SPAN == box_ids, owner_ref[...], 0), axis=1, keepdims=True
    )
    target = lax.rem(owner * SPAN + SPAN // 2 + lax.rem(seg, SPAN), count)
    tile_ids = lax.broadcasted_iota(jnp.int32, (rows, count), 1)
    chosen = jnp.where(target == tile_ids, 1.0, 0.0)
    lower = jnp.where(
        lax.broadcasted_iota(jnp.int32, (rows, rows), 0)
        > lax.broadcasted_iota(jnp.int32, (rows, rows), 1),
        1.0,
        0.0,
    )
    earlier = jnp.dot(lower, chosen, preferred_element_type=jnp.float32)
    rank = jnp.sum(earlier * chosen, axis=1, keepdims=True)
    slots = count * cap
    slot = target.astype(jnp.float32) * cap + rank
    slot_ids = lax.broadcasted_iota(jnp.int32, (rows, slots), 1).astype(jnp.float32)
    place = jnp.where(slot == slot_ids, 1.0, 0.0)
    weighted = regional_ref[...] * weight_ref[...]
    over_rows = (((0,), (0,)), ((), ()))
    outgoing = lax.dot_general(
        place, weighted, over_rows, precision=HIGHEST, preferred_element_type=jnp.float32
    )
    chunks = weighted.shape[1] // depth
    for k in range(chunks):
        send[:, k * cap : (k + 1) * cap, :] = outgoing[:, k * depth : (k + 1) * depth].reshape(
            count, cap, depth
        )
    lane = lax.broadcasted_iota(jnp.int32, (rows, depth), 1)
    lane = (lane - lax.rem(me * cap, depth)).astype(jnp.float32)
    marks = jnp.where(lane == rank, (col_ref[...] + 1).astype(jnp.float32), 0.0)
    columns = lax.dot_general(
        chosen, marks, over_rows, precision=HIGHEST, preferred_element_type=jnp.float32
    )
    send[:, chunks * cap : chunks * cap + 8, :] = jnp.broadcast_to(
        columns[:, None, :], (count, 8, depth)
    )

    pl.semaphore_wait(barrier, count - 1)

    def block_copy(k):
        return pltpu.make_async_remote_copy(
            src_ref=send.at[lax.rem(me + k, count)],
            dst_ref=recv.at[me],
            send_sem=a2a_send.at[k],
            recv_sem=a2a_recv.at[k],
            device_id={"tile": lax.rem(me + k, count)},
            device_id_type=MESH,
        )

    def halo(ref, width, which):
        extent = ref.shape[0]
        to_right = pltpu.make_async_remote_copy(
            src_ref=ref.at[pl.ds(extent - 2 * width, width)],
            dst_ref=ref.at[pl.ds(0, width)],
            send_sem=halo_send.at[2 * which],
            recv_sem=halo_recv.at[2 * which],
            device_id={"tile": right},
            device_id_type=MESH,
        )
        to_left = pltpu.make_async_remote_copy(
            src_ref=ref.at[pl.ds(width, width)],
            dst_ref=ref.at[pl.ds(extent - width, width)],
            send_sem=halo_send.at[2 * which + 1],
            recv_sem=halo_recv.at[2 * which + 1],
            device_id={"tile": left},
            device_id_type=MESH,
        )
        return to_right, to_left

    halos = {
        "now": halo(d0, 2, 0),
        "half": halo(half, 1, 1),
        "bulk": halo(bulk, 1, 2),
        "mat": halo(mat, 3, 3),
        "next": halo(d1, 2, 4),
        "band0": halo(band0, 4, 5),
        "band1": halo(band1, 2, 6),
    }

    def start(*names):
        @pl.when(has_right)
        def _():
            for name in names:
                halos[name][0].start()

        @pl.when(has_left)
        def _():
            for name in names:
                halos[name][1].start()

    def arrive(*names):
        @pl.when(has_left)
        def _():
            for name in names:
                halos[name][0].wait_recv()

        @pl.when(has_right)
        def _():
            for name in names:
                halos[name][1].wait_recv()

    def sent(*names):
        @pl.when(has_right)
        def _():
            for name in names:
                halos[name][0].wait_send()

        @pl.when(has_left)
        def _():
            for name in names:
                halos[name][1].wait_send()

    rims = ((d0, 2), (half, 1), (bulk, 1), (mat, 3), (d1, 2), (band0, 4), (band1, 2))

    @pl.when(jnp.logical_not(has_left))
    def _():
        for ref, width in rims:
            ref[0:width] = jnp.zeros((width,) + ref.shape[1:], jnp.float32)

    @pl.when(jnp.logical_not(has_right))
    def _():
        for ref, width in rims:
            extent = ref.shape[0]
            ref[extent - width : extent] = jnp.zeros((width,) + ref.shape[1:], jnp.float32)

    load_now.wait()
    start("now")

    def launch(k, carry):
        block_copy(k).start()
        return carry

    lax.fori_loop(1, count, launch, 0)
    recv[me] = send[me]
    load_class.wait()

    tables = [
        jnp.broadcast_to(table_ref[k : k + 1, :], (across, table_ref.shape[1])) for k in range(3)
    ]

    def look_up(p, carry):
        ids = cls[p]
        lam, mu, irho = [jnp.take_along_axis(t, ids, axis=1) for t in tables]
        values = (0.5 * mu, 0.25 * (lam + mu), TIME_STEP * irho)
        half[p + 1], bulk[p + 1], inv[p] = values
        for k in range(3):
            mat[p + 3, k, 0:8] = values[k][0:8]
            mat[p + 3, k, 8:16] = values[k][across - 8 : across]
        return carry

    lax.fori_loop(0, planes, look_up, 0)
    start("half", "bulk", "mat")

    def strain(d, p):
        g[p] = volume(d[p + 2, 0], d[p, 0], d[p + 1, 1], d[p + 1, 2], bulk[p])

    def advance(d, p):
        now = [d[p + 2, i] for i in range(3)]
        nxt = [d[p + 3, i] for i in range(3)]
        prv = [d[p + 1, i] for i in range(3)]
        return now, elastic(
            now, nxt, prv, half[p + 1], half[p + 2], half[p], g[p + 1], g[p + 2], g[p]
        )

    def first(p):
        now, forces = advance(d0, p)
        for i in range(3):
            d1[p + 2, i] = 2.0 * now[i] - before[p, i] + inv[p] * forces[i]

    def second(p):
        now, forces = advance(d1, p)
        for i in range(3):
            out_ref[p, i] = 2.0 * now[i] - d0[p + 2, i] + inv[p] * forces[i]

    def sweep(d, update, middle):
        if middle:
            lax.fori_loop(2, planes, lambda p, c: (strain(d, p), c)[1], 0)
            lax.fori_loop(2, planes - 2, lambda p, c: (update(p), c)[1], 0)
        else:
            jump = planes - 2

            lax.fori_loop(
                0, 4, lambda k, c: (strain(d, k + (k // 2) * jump), c)[1], 0
            )
            lax.fori_loop(
                0, 4, lambda k, c: (update(k + (k // 2) * (planes - 4)), c)[1], 0
            )

    load_prev.wait()
    sweep(d0, first, True)
    arrive("now", "half", "bulk")
    sweep(d0, first, False)
    start("next")
    sweep(d1, second, True)

    def land(k, carry):
        block_copy(k).wait_recv()
        return carry

    lax.fori_loop(1, count, land, 0)
    marked = recv[:, chunks * cap : chunks * cap + 8, :]
    row_in = lax.broadcasted_iota(jnp.int32, marked.shape, 1)
    marked = jnp.where(row_in == 0, marked, 0.0)
    group = depth // cap
    parts = [
        jnp.sum(marked[k : k + group].reshape(-1, depth), axis=0, keepdims=True)
        for k in range(0, count, group)
    ]
    sources = jnp.concatenate(parts, axis=1)
    ids = lax.broadcasted_iota(jnp.int32, (planes * 16, 1), 0)
    at, x4 = lax.rem(ids, 16), (ids // 16) * 4 + 1
    wanted = jnp.where(
        at == 1,
        x4,
        jnp.where(at == 2, x4 + 1, jnp.where(at == 13, x4 + 2, jnp.where(at == 14, x4 + 3, -1))),
    ).astype(jnp.float32)
    picks = jnp.where(wanted == sources, 1.0, 0.0)
    for k in range(chunks):
        rows_k = recv[:, k * cap : (k + 1) * cap, :].reshape(slots, depth)
        field = jnp.dot(picks, rows_k, precision=HIGHEST, preferred_element_type=jnp.float32)
        field = field.reshape(planes, 16, depth)
        if k < 3:
            band0[4 : 4 + planes, k] = field
        else:
            band1[2 : 2 + planes, k - 3] = field
    start("band0", "band1")

    arrive("next")
    sweep(d1, second, False)
    arrive("mat", "band0", "band1")

    slab_row = lax.broadcasted_iota(jnp.int32, (16, depth), 0)
    outer = jnp.where(jnp.logical_or(slab_row < 2, slab_row >= 14), 1.0, 0.0)
    inner = 1.0 - outer

    def force(ref, x, m):
        total = None
        for take, keep in ((outer, inner), (inner, -outer)):
            field = [[ref[x + dx, i] * take for i in range(3)] for dx in (-1, 0, 1)]
            far = [ref[x + dx, 0] * take for dx in (-2, 2)]
            g_prv = volume(field[1][0], far[0], field[0][1], field[0][2], mat[m - 1, 1])
            g_now = volume(field[2][0], field[0][0], field[1][1], field[1][2], mat[m, 1])
            g_nxt = volume(far[1], field[1][0], field[2][1], field[2][2], mat[m + 1, 1])
            parts = elastic(
                field[1], field[2], field[0], mat[m, 0], mat[m + 1, 0], mat[m - 1, 0],
                g_now, g_nxt, g_prv,
            )
            parts = [keep * part for part in parts]
            total = parts if total is None else [a + b for a, b in zip(total, parts)]
        return total

    def first_change(q, carry):
        push = force(band0, q + 2, q + 1)
        for i in range(3):
            delta[q, i] = mat[q + 1, 2] * push[i]
        return carry

    lax.fori_loop(0, planes + 4, first_change, 0)

    def slab_strain(q, carry):
        gs[q] = volume(
            delta[q + 2, 0], delta[q, 0], delta[q + 1, 1], delta[q + 1, 2], mat[q + 2, 1]
        )
        return carry

    lax.fori_loop(0, planes + 2, slab_strain, 0)

    def second_change(p, carry):
        push = force(band1, p + 2, p + 3)
        now = [delta[p + 2, i] for i in range(3)]
        nxt = [delta[p + 3, i] for i in range(3)]
        prv = [delta[p + 1, i] for i in range(3)]
        spread = elastic(
            now, nxt, prv, mat[p + 3, 0], mat[p + 4, 0], mat[p + 2, 0],
            gs[p + 1], gs[p + 2], gs[p],
        )
        for i in range(3):
            change = 2.0 * now[i] + mat[p + 3, 2] * (spread[i] + push[i])
            out_ref[p, i, 0:8] += change[0:8]
            out_ref[p, i, across - 8 : across] += change[8:16]
        return carry

    lax.fori_loop(0, planes, second_change, 0)

    sent("now", "half", "bulk", "mat", "next", "band0", "band1")

    def leave(k, carry):
        block_copy(k).wait_send()
        return carry

    lax.fori_loop(1, count, leave, 0)


def shards(
    regional,
    row_weight,
    row_seg,
    row_col,
    box_owner,
    cell_class,
    soil_props,
    build_props,
    real_ids,
    disp_prev,
    disp_now,
):
    count = lax.axis_size("tile")
    planes, _, _, across, depth = disp_now.shape
    capacity = max(2, 2 * regional.shape[0] // count)
    cap = -(-capacity // 8) * 8
    block = 6 * cap + 8
    table = jnp.concatenate([soil_props, build_props[real_ids[0]]], axis=1)
    table = jnp.pad(table, ((0, 5), (0, depth - table.shape[1])))
    plane = (across, depth)
    f32 = jnp.float32
    vmem = pl.BlockSpec(memory_space=pltpu.VMEM)
    hbm = pl.BlockSpec(memory_space=pl.ANY)
    result = pl.pallas_call(
        functools.partial(body, count, cap),
        out_shape=jax.ShapeDtypeStruct((planes, 3) + plane, f32),
        in_specs=[vmem] * 6 + [hbm] * 3,
        out_specs=vmem,
        scratch_shapes=[
            pltpu.VMEM((planes,) + plane, jnp.int32),
            pltpu.VMEM((planes, 3) + plane, f32),
            pltpu.VMEM((planes + 4, 3) + plane, f32),
            pltpu.VMEM((planes + 4, 3) + plane, f32),
            pltpu.VMEM((planes + 2,) + plane, f32),
            pltpu.VMEM((planes + 2,) + plane, f32),
            pltpu.VMEM((planes,) + plane, f32),
            pltpu.VMEM((planes + 2,) + plane, f32),
            pltpu.VMEM((planes + 6, 3, 16, depth), f32),
            pltpu.VMEM((planes + 8, 3, 16, depth), f32),
            pltpu.VMEM((planes + 4, 3, 16, depth), f32),
            pltpu.VMEM((planes + 4, 3, 16, depth), f32),
            pltpu.VMEM((planes + 2, 16, depth), f32),
            pltpu.VMEM((count, block, depth), f32),
            pltpu.VMEM((count, block, depth), f32),
            pltpu.SemaphoreType.DMA((3,)),
            pltpu.SemaphoreType.DMA((count,)),
            pltpu.SemaphoreType.DMA((count,)),
            pltpu.SemaphoreType.DMA((14,)),
            pltpu.SemaphoreType.DMA((14,)),
        ],
        compiler_params=pltpu.CompilerParams(
            collective_id=0, has_side_effects=True, vmem_limit_bytes=56 * 1024 * 1024
        ),
        cost_estimate=pl.CostEstimate(
            flops=200 * planes * across * depth * 3,
            bytes_accessed=40 * planes * across * depth,
            transcendentals=0,
        ),
    )(
        regional,
        row_weight,
        row_seg,
        row_col,
        box_owner[None],
        table,
        cell_class,
        disp_prev.reshape((planes, 3) + plane),
        disp_now.reshape((planes, 3) + plane),
    )
    return result.reshape(disp_now.shape)


def solution(mesh):
    row = P(("scen", "tile"), None)
    cell = P(("scen", "tile"), None, None)
    field = P(("scen", "tile"), None, None, None, None)
    return jax.shard_map(
        shards,
        mesh=mesh,
        in_specs=(row, row, row, row, P("scen"), cell, P(), P(), P("scen"), field, field),
        out_specs=field,
        check_vma=False,
    )
```

```python
import functools

import jax
import jax.numpy as jnp
from jax import lax
from jax.experimental import pallas as pl
from jax.experimental.pallas import tpu as pltpu
from jax.sharding import PartitionSpec as P

SPAN = 4
TIME_STEP = 0.04
HIGHEST = lax.Precision.HIGHEST
MESH = pl.DeviceIdType.MESH


def above(a, axis):
    size = a.shape[axis]
    at = lax.broadcasted_iota(jnp.int32, a.shape, axis)
    return jnp.where(at == size - 1, 0.0, pltpu.roll(a, size - 1, axis))


def below(a, axis, edge=0.0):
    at = lax.broadcasted_iota(jnp.int32, a.shape, axis)
    return jnp.where(at == 0, edge, pltpu.roll(a, 1, axis))


def volume(xp, xm, vy, vz, bulk):
    total = (xp - xm) + (above(vy, 0) - below(vy, 0)) + (above(vz, 1) - below(vz, 1))
    return bulk * total


def elastic(now, nxt, prv, half, half_nxt, half_prv, g, g_nxt, g_prv):
    face_xp = half + half_nxt
    face_xm = half + half_prv
    face_y = half + above(half, 0)
    face_z = half + above(half, 1)
    push = (
        g_nxt - g_prv,
        above(g, 0) - below(g, 0),
        above(g, 1) - below(g, 1),
    )
    result = []
    for i in range(3):
        v = now[i]
        total = face_xp * (nxt[i] - v) - face_xm * (v - prv[i])
        edge = half * v
        for axis, face in ((0, face_y), (1, face_z)):
            flow = face * (above(v, axis) - v)
            total = total + (flow - below(flow, axis, edge))
        result.append(total + push[i])
    return result


def body(
    count,
    cap,
    regional_ref,
    weight_ref,
    seg_ref,
    col_ref,
    owner_ref,
    soil_ref,
    build_ref,
    real_ref,
    class_ref,
    prev_ref,
    now_ref,
    out_ref,
    cls,
    slab_cls,
    before,
    d0,
    d1,
    half,
    bulk,
    inv,
    g,
    mat,
    band0,
    band1,
    edge_out,
    edge_in,
    delta,
    gs,
    send,
    recv,
    local_sem,
    a2a_send,
    a2a_recv,
    halo_send,
    halo_recv,
):
    me = lax.axis_index("tile")
    position = lax.rem(me + count - SPAN // 2, SPAN)
    right = lax.rem(me + 1, count)
    left = lax.rem(me + count - 1, count)
    planes, across, depth = inv.shape
    has_left, has_right = position > 0, position < SPAN - 1

    load_now = pltpu.make_async_copy(now_ref, d0.at[pl.ds(2, planes)], local_sem.at[0])
    load_class = pltpu.make_async_copy(class_ref, cls.at[pl.ds(1, planes)], local_sem.at[1])
    load_low = pltpu.make_async_copy(
        class_ref.at[:, pl.ds(0, 8)], slab_cls.at[pl.ds(3, planes), pl.ds(0, 8)], local_sem.at[3]
    )
    load_high = pltpu.make_async_copy(
        class_ref.at[:, pl.ds(across - 8, 8)],
        slab_cls.at[pl.ds(3, planes), pl.ds(8, 8)],
        local_sem.at[4],
    )
    load_prev = pltpu.make_async_copy(prev_ref, before, local_sem.at[2])
    load_low.start()
    load_high.start()
    load_class.start()
    load_now.start()
    load_prev.start()

    barrier = pltpu.get_barrier_semaphore()

    def greet(k, carry):
        pl.semaphore_signal(
            barrier, inc=1, device_id={"tile": lax.rem(me + k, count)}, device_id_type=MESH
        )
        return carry

    lax.fori_loop(1, count, greet, 0)

    rows = regional_ref.shape[0]
    boxes = owner_ref.shape[1]
    seg = seg_ref[...]
    owner = jnp.zeros_like(seg)
    for box in range(boxes):
        owner = jnp.where(seg // SPAN == box, owner_ref[0, box], owner)
    target = lax.rem(owner * SPAN + SPAN // 2 + lax.rem(seg, SPAN), count)
    tile_ids = lax.broadcasted_iota(jnp.int32, (count, rows), 0)
    chosen = jnp.where(target == tile_ids, 1.0, 0.0)
    upper = jnp.where(
        lax.broadcasted_iota(jnp.int32, (rows, rows), 0)
        < lax.broadcasted_iota(jnp.int32, (rows, rows), 1),
        1.0,
        0.0,
    )
    earlier = jnp.dot(chosen, upper, preferred_element_type=jnp.float32)
    rank = jnp.sum(earlier * chosen, axis=0, keepdims=True)
    slots = count * cap
    slot = target.astype(jnp.float32) * cap + rank
    slot_ids = lax.broadcasted_iota(jnp.int32, (slots, rows), 0).astype(jnp.float32)
    place = jnp.where(slot == slot_ids, weight_ref[...], 0.0)
    outgoing = jnp.dot(
        place, regional_ref[...], precision=HIGHEST, preferred_element_type=jnp.float32
    )
    chunks = regional_ref.shape[1] // depth
    for k in range(chunks):
        send[:, k * cap : (k + 1) * cap, :] = outgoing[:, k * depth : (k + 1) * depth].reshape(
            count, cap, depth
        )
    lane = lax.broadcasted_iota(jnp.int32, (depth, rows), 0)
    lane = (lane - lax.rem(me * cap, depth)).astype(jnp.float32)
    marks = jnp.where(lane == rank, 1.0, 0.0)
    columns = lax.dot_general(
        chosen * (col_ref[...] + 1).astype(jnp.float32),
        marks,
        (((1,), (1,)), ((), ())),
        precision=HIGHEST,
        preferred_element_type=jnp.float32,
    )
    send[:, chunks * cap : chunks * cap + 8, :] = jnp.broadcast_to(
        columns[:, None, :], (count, 8, depth)
    )

    pl.semaphore_wait(barrier, count - 1)

    def block_copy(k):
        return pltpu.make_async_remote_copy(
            src_ref=send.at[lax.rem(me + k, count)],
            dst_ref=recv.at[me],
            send_sem=a2a_send.at[k],
            recv_sem=a2a_recv.at[k],
            device_id={"tile": lax.rem(me + k, count)},
            device_id_type=MESH,
        )

    def pair(which, from_low, to_high, from_high, to_low):
        to_right = pltpu.make_async_remote_copy(
            src_ref=from_high,
            dst_ref=to_low,
            send_sem=halo_send.at[2 * which],
            recv_sem=halo_recv.at[2 * which],
            device_id={"tile": right},
            device_id_type=MESH,
        )
        to_left = pltpu.make_async_remote_copy(
            src_ref=from_low,
            dst_ref=to_high,
            send_sem=halo_send.at[2 * which + 1],
            recv_sem=halo_recv.at[2 * which + 1],
            device_id={"tile": left},
            device_id_type=MESH,
        )
        return to_right, to_left

    def halo(ref, width, which):
        extent = ref.shape[0]
        spans = [width, extent - width, extent - 2 * width, 0]
        return pair(which, *[ref.at[pl.ds(at, width)] for at in spans])

    def near(d, which):
        return pair(which, d.at[2], d.at[planes + 2], d.at[planes + 1], d.at[1])

    def far(d, which):
        return pair(which, d.at[3, 0], d.at[planes + 3, 0], d.at[planes, 0], d.at[0, 0])

    halos = {
        "class": halo(cls, 1, 0),
        "slab": halo(slab_cls, 3, 1),
        "near0": near(d0, 2),
        "far0": far(d0, 3),
        "near1": near(d1, 4),
        "far1": far(d1, 5),
        "edge": pair(6, edge_out.at[0], edge_in.at[1], edge_out.at[1], edge_in.at[0]),
    }

    def start(*names):
        @pl.when(has_right)
        def _():
            for name in names:
                halos[name][0].start()

        @pl.when(has_left)
        def _():
            for name in names:
                halos[name][1].start()

    def arrive(*names):
        @pl.when(has_left)
        def _():
            for name in names:
                halos[name][0].wait_recv()

        @pl.when(has_right)
        def _():
            for name in names:
                halos[name][1].wait_recv()

    def sent(*names):
        @pl.when(has_right)
        def _():
            for name in names:
                halos[name][0].wait_send()

        @pl.when(has_left)
        def _():
            for name in names:
                halos[name][1].wait_send()

    rims = ((d0, 2), (half, 1), (bulk, 1), (mat, 3), (d1, 2), (edge_in, 1))

    @pl.when(jnp.logical_not(has_left))
    def _():
        for ref, width in rims:
            ref[0:width] = jnp.zeros((width,) + ref.shape[1:], jnp.float32)

    @pl.when(jnp.logical_not(has_right))
    def _():
        for ref, width in rims:
            extent = ref.shape[0]
            ref[extent - width : extent] = jnp.zeros((width,) + ref.shape[1:], jnp.float32)

    load_low.wait()
    load_high.wait()
    load_class.wait()
    load_now.wait()
    start("class", "slab", "near0", "far0")

    def launch(k, carry):
        block_copy(k).start()
        return carry

    lax.fori_loop(1, count, launch, 0)
    recv[me] = send[me]

    entry = lax.broadcasted_iota(jnp.int32, build_ref.shape[1:], 0) == real_ref[0]
    tables = []
    for k in range(3):
        chosen_build = jnp.sum(jnp.where(entry, build_ref[k], 0.0), axis=0, keepdims=True)
        both = jnp.concatenate([soil_ref[k : k + 1, :], chosen_build], axis=1)
        blank = jnp.zeros((1, depth - both.shape[1]), jnp.float32)
        both = jnp.concatenate([both, blank], axis=1)
        tables.append(jnp.broadcast_to(both, (across, depth)))

    def properties(ids):
        lam, mu, irho = [
            jnp.take_along_axis(t[0 : ids.shape[0]], ids, axis=1) for t in tables
        ]
        return 0.5 * mu, 0.25 * (lam + mu), TIME_STEP * irho

    def look_up(p, carry):
        half[p + 1], bulk[p + 1], inv[p] = properties(cls[p + 1])
        return carry

    def look_up_rim(e):
        half[e], bulk[e], _ = properties(cls[e])

    def look_up_slab(e, carry):
        mat[e, 0], mat[e, 1], mat[e, 2] = properties(slab_cls[e])
        return carry

    lax.fori_loop(0, planes, look_up, 0)
    lax.fori_loop(3, planes + 3, look_up_slab, 0)

    def strain(d, p):
        g[p] = volume(d[p + 2, 0], d[p, 0], d[p + 1, 1], d[p + 1, 2], bulk[p])

    def advance(d, p):
        now = [d[p + 2, i] for i in range(3)]
        nxt = [d[p + 3, i] for i in range(3)]
        prv = [d[p + 1, i] for i in range(3)]
        return now, elastic(
            now, nxt, prv, half[p + 1], half[p + 2], half[p], g[p + 1], g[p + 2], g[p]
        )

    def first(p):
        now, forces = advance(d0, p)
        for i in range(3):
            d1[p + 2, i] = 2.0 * now[i] - before[p, i] + inv[p] * forces[i]

    def second(p):
        now, forces = advance(d1, p)
        for i in range(3):
            out_ref[p, i] = 2.0 * now[i] - d0[p + 2, i] + inv[p] * forces[i]

    def sweep(d, update, middle):
        if middle:
            lax.fori_loop(2, planes, lambda p, c: (strain(d, p), c)[1], 0)
            lax.fori_loop(2, planes - 2, lambda p, c: (update(p), c)[1], 0)
        else:
            jump = planes - 2

            lax.fori_loop(
                0, 4, lambda k, c: (strain(d, k + (k // 2) * jump), c)[1], 0
            )
            lax.fori_loop(
                0, 4, lambda k, c: (update(k + (k // 2) * (planes - 4)), c)[1], 0
            )

    load_prev.wait()
    sweep(d0, first, True)
    arrive("class", "slab", "near0", "far0")

    @pl.when(has_left)
    def _():
        look_up_rim(0)
        lax.fori_loop(0, 3, look_up_slab, 0)

    @pl.when(has_right)
    def _():
        look_up_rim(planes + 1)
        lax.fori_loop(planes + 3, planes + 6, look_up_slab, 0)

    sweep(d0, first, False)
    start("near1", "far1")
    sweep(d1, second, True)

    def land(k, carry):
        block_copy(k).wait_recv()
        return carry

    lax.fori_loop(1, count, land, 0)
    marked = recv[:, chunks * cap : chunks * cap + 8, :]
    row_in = lax.broadcasted_iota(jnp.int32, marked.shape, 1)
    marked = jnp.where(row_in == 0, marked, 0.0)
    group = depth // cap
    parts = [
        jnp.sum(marked[k : k + group].reshape(-1, depth), axis=0, keepdims=True)
        for k in range(0, count, group)
    ]
    sources = jnp.concatenate(parts, axis=1)
    ids = lax.broadcasted_iota(jnp.int32, (planes * 16, 1), 0)
    at, x4 = lax.rem(ids, 16), (ids // 16) * 4 + 1
    wanted = jnp.where(
        at == 1,
        x4,
        jnp.where(at == 2, x4 + 1, jnp.where(at == 13, x4 + 2, jnp.where(at == 14, x4 + 3, -1))),
    ).astype(jnp.float32)
    rim = lax.broadcasted_iota(jnp.int32, (32, 1), 0)
    rim = (rim + (rim // 16) * (4 * planes - 32) + 1).astype(jnp.float32)
    picks = jnp.where(jnp.concatenate([wanted, rim], axis=0) == sources, 1.0, 0.0)
    for k in range(chunks):
        rows_k = recv[:, k * cap : (k + 1) * cap, :].reshape(slots, depth)
        field = jnp.dot(picks, rows_k, precision=HIGHEST, preferred_element_type=jnp.float32)
        edge_out[0, k] = field[planes * 16 : planes * 16 + 16]
        edge_out[1, k] = field[planes * 16 + 16 : planes * 16 + 32]
        field = field[0 : planes * 16].reshape(planes, 16, depth)
        if k < 3:
            band0[4 : 4 + planes, k] = field
        else:
            band1[2 : 2 + planes, k - 3] = field
    start("edge")

    arrive("near1", "far1")
    sweep(d1, second, False)
    arrive("edge")
    spread = jnp.where(
        wanted[0:64]
        == (lax.broadcasted_iota(jnp.int32, (1, 16), 1) + 1).astype(jnp.float32),
        1.0,
        0.0,
    )
    for side in range(2):
        for k in range(chunks):
            field = jnp.dot(
                spread, edge_in[side, k], precision=HIGHEST, preferred_element_type=jnp.float32
            ).reshape(4, 16, depth)
            if k < 3:
                at_plane = side * (planes + 4)
                band0[at_plane : at_plane + 4, k] = field
            else:
                at_plane = side * (planes + 2)
                band1[at_plane : at_plane + 2, k - 3] = field[0:2] if side else field[2:4]

    slab_row = lax.broadcasted_iota(jnp.int32, (16, depth), 0)
    outer = jnp.where(jnp.logical_or(slab_row < 2, slab_row >= 14), 1.0, 0.0)
    inner = 1.0 - outer

    def force(ref, x, m):
        total = None
        for take, keep in ((outer, inner), (inner, -outer)):
            field = [[ref[x + dx, i] * take for i in range(3)] for dx in (-1, 0, 1)]
            far = [ref[x + dx, 0] * take for dx in (-2, 2)]
            g_prv = volume(field[1][0], far[0], field[0][1], field[0][2], mat[m - 1, 1])
            g_now = volume(field[2][0], field[0][0], field[1][1], field[1][2], mat[m, 1])
            g_nxt = volume(far[1], field[1][0], field[2][1], field[2][2], mat[m + 1, 1])
            parts = elastic(
                field[1], field[2], field[0], mat[m, 0], mat[m + 1, 0], mat[m - 1, 0],
                g_now, g_nxt, g_prv,
            )
            parts = [keep * part for part in parts]
            total = parts if total is None else [a + b for a, b in zip(total, parts)]
        return total

    def first_change(q, carry):
        push = force(band0, q + 2, q + 1)
        for i in range(3):
            delta[q, i] = mat[q + 1, 2] * push[i]
        return carry

    lax.fori_loop(0, planes + 4, first_change, 0)

    def slab_strain(q, carry):
        gs[q] = volume(
            delta[q + 2, 0], delta[q, 0], delta[q + 1, 1], delta[q + 1, 2], mat[q + 2, 1]
        )
        return carry

    lax.fori_loop(0, planes + 2, slab_strain, 0)

    def second_change(p, carry):
        push = force(band1, p + 2, p + 3)
        now = [delta[p + 2, i] for i in range(3)]
        nxt = [delta[p + 3, i] for i in range(3)]
        prv = [delta[p + 1, i] for i in range(3)]
        spread = elastic(
            now, nxt, prv, mat[p + 3, 0], mat[p + 4, 0], mat[p + 2, 0],
            gs[p + 1], gs[p + 2], gs[p],
        )
        for i in range(3):
            change = 2.0 * now[i] + mat[p + 3, 2] * (spread[i] + push[i])
            out_ref[p, i, 0:8] += change[0:8]
            out_ref[p, i, across - 8 : across] += change[8:16]
        return carry

    lax.fori_loop(0, planes, second_change, 0)

    sent("class", "slab", "near0", "far0", "near1", "far1", "edge")

    def leave(k, carry):
        block_copy(k).wait_send()
        return carry

    lax.fori_loop(1, count, leave, 0)


def shards(
    regional,
    row_weight,
    row_seg,
    row_col,
    box_owner,
    cell_class,
    soil_props,
    build_props,
    real_ids,
    disp_prev,
    disp_now,
):
    count = lax.axis_size("tile")
    planes, _, _, across, depth = disp_now.shape
    capacity = max(2, 2 * regional.shape[0] // count)
    cap = -(-capacity // 8) * 8
    block = 6 * cap + 8
    plane = (across, depth)
    f32 = jnp.float32
    vmem = pl.BlockSpec(memory_space=pltpu.VMEM)
    smem = pl.BlockSpec(memory_space=pltpu.SMEM)
    hbm = pl.BlockSpec(memory_space=pl.ANY)
    result = pl.pallas_call(
        functools.partial(body, count, cap),
        out_shape=jax.ShapeDtypeStruct((planes, 3) + plane, f32),
        in_specs=[vmem] * 4 + [smem] + [vmem] * 2 + [smem] + [hbm] * 3,
        out_specs=vmem,
        scratch_shapes=[
            pltpu.VMEM((planes + 2,) + plane, jnp.int32),
            pltpu.VMEM((planes + 6, 16, depth), jnp.int32),
            pltpu.VMEM((planes, 3) + plane, f32),
            pltpu.VMEM((planes + 4, 3) + plane, f32),
            pltpu.VMEM((planes + 4, 3) + plane, f32),
            pltpu.VMEM((planes + 2,) + plane, f32),
            pltpu.VMEM((planes + 2,) + plane, f32),
            pltpu.VMEM((planes,) + plane, f32),
            pltpu.VMEM((planes + 2,) + plane, f32),
            pltpu.VMEM((planes + 6, 3, 16, depth), f32),
            pltpu.VMEM((planes + 8, 3, 16, depth), f32),
            pltpu.VMEM((planes + 4, 3, 16, depth), f32),
            pltpu.VMEM((2, 6, 16, depth), f32),
            pltpu.VMEM((2, 6, 16, depth), f32),
            pltpu.VMEM((planes + 4, 3, 16, depth), f32),
            pltpu.VMEM((planes + 2, 16, depth), f32),
            pltpu.VMEM((count, block, depth), f32),
            pltpu.VMEM((count, block, depth), f32),
            pltpu.SemaphoreType.DMA((5,)),
            pltpu.SemaphoreType.DMA((count,)),
            pltpu.SemaphoreType.DMA((count,)),
            pltpu.SemaphoreType.DMA((14,)),
            pltpu.SemaphoreType.DMA((14,)),
        ],
        compiler_params=pltpu.CompilerParams(
            collective_id=0, has_side_effects=True, vmem_limit_bytes=56 * 1024 * 1024
        ),
        cost_estimate=pl.CostEstimate(
            flops=200 * planes * across * depth * 3,
            bytes_accessed=40 * planes * across * depth,
            transcendentals=0,
        ),
    )(
        regional,
        row_weight.reshape(1, -1),
        row_seg.reshape(1, -1),
        row_col.reshape(1, -1),
        box_owner[None],
        soil_props,
        jnp.transpose(build_props, (1, 0, 2)),
        real_ids,
        cell_class,
        disp_prev.reshape((planes, 3) + plane),
        disp_now.reshape((planes, 3) + plane),
    )
    return result.reshape(disp_now.shape)


def solution(mesh):
    row = P(("scen", "tile"), None)
    cell = P(("scen", "tile"), None, None)
    field = P(("scen", "tile"), None, None, None, None)
    return jax.shard_map(
        shards,
        mesh=mesh,
        in_specs=(row, row, row, row, P("scen"), cell, P(), P(), P("scen"), field, field),
        out_specs=field,
        check_vma=False,
    )
```

```python
import functools

import jax
import jax.numpy as jnp
from jax import lax
from jax.experimental import pallas as pl
from jax.experimental.pallas import tpu as pltpu
from jax.sharding import PartitionSpec as P

SPAN = 4
TIME_STEP = 0.04
HIGHEST = lax.Precision.HIGHEST
MESH = pl.DeviceIdType.MESH


def above(a, axis):
    size = a.shape[axis]
    at = lax.broadcasted_iota(jnp.int32, a.shape, axis)
    return jnp.where(at == size - 1, 0.0, pltpu.roll(a, size - 1, axis))


def below(a, axis, edge=0.0):
    at = lax.broadcasted_iota(jnp.int32, a.shape, axis)
    return jnp.where(at == 0, edge, pltpu.roll(a, 1, axis))


def volume(xp, xm, vy, vz, bulk):
    total = (xp - xm) + (above(vy, 0) - below(vy, 0)) + (above(vz, 1) - below(vz, 1))
    return bulk * total


def elastic(now, nxt, prv, half, half_nxt, half_prv, g, g_nxt, g_prv):
    face_xp = half + half_nxt
    face_xm = half + half_prv
    face_y = half + above(half, 0)
    face_z = half + above(half, 1)
    push = (
        g_nxt - g_prv,
        above(g, 0) - below(g, 0),
        above(g, 1) - below(g, 1),
    )
    result = []
    for i in range(3):
        v = now[i]
        total = face_xp * (nxt[i] - v) - face_xm * (v - prv[i])
        edge = half * v
        for axis, face in ((0, face_y), (1, face_z)):
            flow = face * (above(v, axis) - v)
            total = total + (flow - below(flow, axis, edge))
        result.append(total + push[i])
    return result


def body(
    count,
    cap,
    regional_ref,
    weight_ref,
    seg_ref,
    col_ref,
    owner_ref,
    soil_ref,
    build_ref,
    real_ref,
    class_ref,
    prev_ref,
    now_ref,
    out_ref,
    cls,
    slab_cls,
    before,
    d0,
    d1,
    half,
    bulk,
    inv,
    g,
    mat,
    band0,
    band1,
    edge_out,
    edge_in,
    delta,
    gs,
    send,
    recv,
    local_sem,
    a2a_send,
    a2a_recv,
    halo_send,
    halo_recv,
):
    me = lax.axis_index("tile")
    position = lax.rem(me + count - SPAN // 2, SPAN)
    right = lax.rem(me + 1, count)
    left = lax.rem(me + count - 1, count)
    planes, across, depth = inv.shape
    has_left, has_right = position > 0, position < SPAN - 1

    load_now = pltpu.make_async_copy(now_ref, d0.at[pl.ds(2, planes)], local_sem.at[0])
    load_class = pltpu.make_async_copy(class_ref, cls.at[pl.ds(1, planes)], local_sem.at[1])
    load_low = pltpu.make_async_copy(
        class_ref.at[:, pl.ds(0, 8)], slab_cls.at[pl.ds(3, planes), pl.ds(0, 8)], local_sem.at[3]
    )
    load_high = pltpu.make_async_copy(
        class_ref.at[:, pl.ds(across - 8, 8)],
        slab_cls.at[pl.ds(3, planes), pl.ds(8, 8)],
        local_sem.at[4],
    )
    load_prev = pltpu.make_async_copy(prev_ref, before, local_sem.at[2])
    load_low.start()
    load_high.start()
    load_class.start()
    load_now.start()
    load_prev.start()

    barrier = pltpu.get_barrier_semaphore()

    def greet(k, carry):
        pl.semaphore_signal(
            barrier, inc=1, device_id={"tile": lax.rem(me + k, count)}, device_id_type=MESH
        )
        return carry

    lax.fori_loop(1, count, greet, 0)

    rows = regional_ref.shape[0]
    boxes = owner_ref.shape[1]
    seg = seg_ref[...]
    owner = jnp.zeros_like(seg)
    for box in range(boxes):
        owner = jnp.where(seg // SPAN == box, owner_ref[0, box], owner)
    target = lax.rem(owner * SPAN + SPAN // 2 + lax.rem(seg, SPAN), count)
    tile_ids = lax.broadcasted_iota(jnp.int32, (count, rows), 0)
    chosen = jnp.where(target == tile_ids, 1.0, 0.0)
    upper = jnp.where(
        lax.broadcasted_iota(jnp.int32, (rows, rows), 0)
        < lax.broadcasted_iota(jnp.int32, (rows, rows), 1),
        1.0,
        0.0,
    )
    earlier = jnp.dot(chosen, upper, preferred_element_type=jnp.float32)
    rank = jnp.sum(earlier * chosen, axis=0, keepdims=True)
    slots = count * cap
    slot = target.astype(jnp.float32) * cap + rank
    slot_ids = lax.broadcasted_iota(jnp.int32, (slots, rows), 0).astype(jnp.float32)
    place = jnp.where(slot == slot_ids, weight_ref[...], 0.0)
    outgoing = jnp.dot(
        place, regional_ref[...], precision=HIGHEST, preferred_element_type=jnp.float32
    )
    chunks = regional_ref.shape[1] // depth
    for k in range(chunks):
        send[:, k * cap : (k + 1) * cap, :] = outgoing[:, k * depth : (k + 1) * depth].reshape(
            count, cap, depth
        )
    lane = lax.broadcasted_iota(jnp.int32, (depth, rows), 0)
    lane = (lane - lax.rem(me * cap, depth)).astype(jnp.float32)
    marks = jnp.where(lane == rank, 1.0, 0.0)
    columns = lax.dot_general(
        chosen * (col_ref[...] + 1).astype(jnp.float32),
        marks,
        (((1,), (1,)), ((), ())),
        precision=HIGHEST,
        preferred_element_type=jnp.float32,
    )
    send[:, chunks * cap : chunks * cap + 8, :] = jnp.broadcast_to(
        columns[:, None, :], (count, 8, depth)
    )

    pl.semaphore_wait(barrier, count - 1)

    def block_copy(k):
        return pltpu.make_async_remote_copy(
            src_ref=send.at[lax.rem(me + k, count)],
            dst_ref=recv.at[me],
            send_sem=a2a_send.at[k],
            recv_sem=a2a_recv.at[k],
            device_id={"tile": lax.rem(me + k, count)},
            device_id_type=MESH,
        )

    def pair(which, from_low, to_high, from_high, to_low):
        to_right = pltpu.make_async_remote_copy(
            src_ref=from_high,
            dst_ref=to_low,
            send_sem=halo_send.at[2 * which],
            recv_sem=halo_recv.at[2 * which],
            device_id={"tile": right},
            device_id_type=MESH,
        )
        to_left = pltpu.make_async_remote_copy(
            src_ref=from_low,
            dst_ref=to_high,
            send_sem=halo_send.at[2 * which + 1],
            recv_sem=halo_recv.at[2 * which + 1],
            device_id={"tile": left},
            device_id_type=MESH,
        )
        return to_right, to_left

    def halo(ref, width, which):
        extent = ref.shape[0]
        spans = [width, extent - width, extent - 2 * width, 0]
        return pair(which, *[ref.at[pl.ds(at, width)] for at in spans])

    def near(d, which):
        return pair(which, d.at[2], d.at[planes + 2], d.at[planes + 1], d.at[1])

    def far(d, which):
        return pair(which, d.at[3, 0], d.at[planes + 3, 0], d.at[planes, 0], d.at[0, 0])

    halos = {
        "class": halo(cls, 1, 0),
        "slab": halo(slab_cls, 3, 1),
        "near0": near(d0, 2),
        "far0": far(d0, 3),
        "near1": near(d1, 4),
        "far1": far(d1, 5),
        "edge": pair(6, edge_out.at[0], edge_in.at[1], edge_out.at[1], edge_in.at[0]),
    }

    def start(*names):
        @pl.when(has_right)
        def _():
            for name in names:
                halos[name][0].start()

        @pl.when(has_left)
        def _():
            for name in names:
                halos[name][1].start()

    def arrive(*names):
        @pl.when(has_left)
        def _():
            for name in names:
                halos[name][0].wait_recv()

        @pl.when(has_right)
        def _():
            for name in names:
                halos[name][1].wait_recv()

    def sent(*names):
        @pl.when(has_right)
        def _():
            for name in names:
                halos[name][0].wait_send()

        @pl.when(has_left)
        def _():
            for name in names:
                halos[name][1].wait_send()

    rims = ((d0, 2), (half, 1), (bulk, 1), (mat, 3), (d1, 2), (edge_in, 1))

    @pl.when(jnp.logical_not(has_left))
    def _():
        for ref, width in rims:
            ref[0:width] = jnp.zeros((width,) + ref.shape[1:], jnp.float32)

    @pl.when(jnp.logical_not(has_right))
    def _():
        for ref, width in rims:
            extent = ref.shape[0]
            ref[extent - width : extent] = jnp.zeros((width,) + ref.shape[1:], jnp.float32)

    load_low.wait()
    load_high.wait()
    load_class.wait()
    load_now.wait()
    start("class", "slab", "near0", "far0")

    def launch(k, carry):
        block_copy(k).start()
        return carry

    lax.fori_loop(1, count, launch, 0)
    recv[me] = send[me]

    entry = lax.broadcasted_iota(jnp.int32, build_ref.shape[1:], 0) == real_ref[0]
    tables = []
    for k in range(3):
        chosen_build = jnp.sum(jnp.where(entry, build_ref[k], 0.0), axis=0, keepdims=True)
        both = jnp.concatenate([soil_ref[k : k + 1, :], chosen_build], axis=1)
        blank = jnp.zeros((1, depth - both.shape[1]), jnp.float32)
        both = jnp.concatenate([both, blank], axis=1)
        tables.append(jnp.broadcast_to(both, (across, depth)))

    def properties(ids):
        lam, mu, irho = [
            jnp.take_along_axis(t[0 : ids.shape[0]], ids, axis=1) for t in tables
        ]
        return 0.5 * mu, 0.25 * (lam + mu), TIME_STEP * irho

    def look_up(p, carry):
        half[p + 1], bulk[p + 1], inv[p] = properties(cls[p + 1])
        return carry

    def look_up_rim(e):
        half[e], bulk[e], _ = properties(cls[e])

    def look_up_slab(e, carry):
        mat[e, 0], mat[e, 1], mat[e, 2] = properties(slab_cls[e])
        return carry

    lax.fori_loop(0, planes, look_up, 0)
    lax.fori_loop(3, planes + 3, look_up_slab, 0)

    def strain(d, p):
        g[p] = volume(d[p + 2, 0], d[p, 0], d[p + 1, 1], d[p + 1, 2], bulk[p])

    def advance(d, p):
        now = [d[p + 2, i] for i in range(3)]
        nxt = [d[p + 3, i] for i in range(3)]
        prv = [d[p + 1, i] for i in range(3)]
        return now, elastic(
            now, nxt, prv, half[p + 1], half[p + 2], half[p], g[p + 1], g[p + 2], g[p]
        )

    def first(p):
        now, forces = advance(d0, p)
        for i in range(3):
            d1[p + 2, i] = 2.0 * now[i] - before[p, i] + inv[p] * forces[i]

    def second(p):
        now, forces = advance(d1, p)
        for i in range(3):
            out_ref[p, i] = 2.0 * now[i] - d0[p + 2, i] + inv[p] * forces[i]

    def sweep(d, update, middle):
        if middle:
            lax.fori_loop(2, planes, lambda p, c: (strain(d, p), c)[1], 0)
            lax.fori_loop(2, planes - 2, lambda p, c: (update(p), c)[1], 0)
        else:
            jump = planes - 2

            lax.fori_loop(
                0, 4, lambda k, c: (strain(d, k + (k // 2) * jump), c)[1], 0
            )
            lax.fori_loop(
                0, 4, lambda k, c: (update(k + (k // 2) * (planes - 4)), c)[1], 0
            )

    load_prev.wait()
    sweep(d0, first, True)
    arrive("class", "slab", "near0", "far0")

    @pl.when(has_left)
    def _():
        look_up_rim(0)
        lax.fori_loop(0, 3, look_up_slab, 0)

    @pl.when(has_right)
    def _():
        look_up_rim(planes + 1)
        lax.fori_loop(planes + 3, planes + 6, look_up_slab, 0)

    sweep(d0, first, False)
    start("near1", "far1")
    sweep(d1, second, True)

    def land(k, carry):
        block_copy(k).wait_recv()
        return carry

    lax.fori_loop(1, count, land, 0)
    marked = recv[:, chunks * cap : chunks * cap + 8, :]
    row_in = lax.broadcasted_iota(jnp.int32, marked.shape, 1)
    marked = jnp.where(row_in == 0, marked, 0.0)
    group = depth // cap
    parts = [
        jnp.sum(marked[k : k + group].reshape(-1, depth), axis=0, keepdims=True)
        for k in range(0, count, group)
    ]
    sources = jnp.concatenate(parts, axis=1)
    ids = lax.broadcasted_iota(jnp.int32, (planes * 16, 1), 0)
    at, x4 = lax.rem(ids, 16), (ids // 16) * 4 + 1
    wanted = jnp.where(
        at == 2,
        x4,
        jnp.where(at == 1, x4 + 1, jnp.where(at == 14, x4 + 2, jnp.where(at == 13, x4 + 3, -1))),
    ).astype(jnp.float32)
    rim = lax.broadcasted_iota(jnp.int32, (32, 1), 0)
    rim = (rim + (rim // 16) * (4 * planes - 32) + 1).astype(jnp.float32)
    picks = jnp.where(jnp.concatenate([wanted, rim], axis=0) == sources, 1.0, 0.0)
    for k in range(chunks):
        rows_k = recv[:, k * cap : (k + 1) * cap, :].reshape(slots, depth)
        field = jnp.dot(picks, rows_k, precision=HIGHEST, preferred_element_type=jnp.float32)
        edge_out[0, k] = field[planes * 16 : planes * 16 + 16]
        edge_out[1, k] = field[planes * 16 + 16 : planes * 16 + 32]
        field = field[0 : planes * 16].reshape(planes, 16, depth)
        if k < 3:
            band0[4 : 4 + planes, k] = field
        else:
            band1[2 : 2 + planes, k - 3] = field
    start("edge")

    arrive("near1", "far1")
    sweep(d1, second, False)
    arrive("edge")
    spread = jnp.where(
        wanted[0:64]
        == (lax.broadcasted_iota(jnp.int32, (1, 16), 1) + 1).astype(jnp.float32),
        1.0,
        0.0,
    )
    for side in range(2):
        for k in range(chunks):
            field = jnp.dot(
                spread, edge_in[side, k], precision=HIGHEST, preferred_element_type=jnp.float32
            ).reshape(4, 16, depth)
            if k < 3:
                at_plane = side * (planes + 4)
                band0[at_plane : at_plane + 4, k] = field
            else:
                at_plane = side * (planes + 2)
                band1[at_plane : at_plane + 2, k - 3] = field[0:2] if side else field[2:4]

    slab_row = lax.broadcasted_iota(jnp.int32, (16, depth), 0)
    outside = jnp.logical_or(slab_row < 2, slab_row >= 14)
    sign = jnp.where(outside, -1.0, 1.0)
    downward = lax.rem(slab_row, 12) == 1
    turn = jnp.where(downward, 1.0, -1.0)

    def across_to(a):
        return jnp.where(downward, pltpu.roll(a, 15, 0), pltpu.roll(a, 1, 0))

    def force(ref, x, m):
        fields = [[sign * ref[x + dx, i] for i in range(3)] for dx in (-1, 0, 1)]
        prv, now, nxt = fields
        g_prv, g_now, g_nxt = [
            turn * mat[m + dx, 1] * fields[dx + 1][1] for dx in (-1, 0, 1)
        ]
        face = mat[m, 0] + across_to(mat[m, 0])
        source = (nxt[0] - prv[0]) + (above(now[2], 1) - below(now[2], 1))
        source = turn * across_to(mat[m, 1]) * source
        reach = mat[m, 1] * now[1]
        reach = pltpu.roll(jnp.where(downward, reach, 0.0), 15, 0) + pltpu.roll(
            jnp.where(downward, 0.0, reach), 1, 0
        )
        return (
            face * now[0] + (g_nxt - g_prv),
            face * now[1] + source + reach,
            face * now[2] + (above(g_now, 1) - below(g_now, 1)),
        )

    def first_change(q, carry):
        push = force(band0, q + 2, q + 1)
        for i in range(3):
            delta[q, i] = mat[q + 1, 2] * push[i]
        return carry

    lax.fori_loop(0, planes + 4, first_change, 0)

    def slab_strain(q, carry):
        gs[q] = volume(
            delta[q + 2, 0], delta[q, 0], delta[q + 1, 1], delta[q + 1, 2], mat[q + 2, 1]
        )
        return carry

    lax.fori_loop(0, planes + 2, slab_strain, 0)

    def second_change(p, carry):
        push = force(band1, p + 2, p + 3)
        now = [delta[p + 2, i] for i in range(3)]
        nxt = [delta[p + 3, i] for i in range(3)]
        prv = [delta[p + 1, i] for i in range(3)]
        spread = elastic(
            now, nxt, prv, mat[p + 3, 0], mat[p + 4, 0], mat[p + 2, 0],
            gs[p + 1], gs[p + 2], gs[p],
        )
        for i in range(3):
            change = 2.0 * now[i] + mat[p + 3, 2] * (spread[i] + push[i])
            out_ref[p, i, 0:8] += change[0:8]
            out_ref[p, i, across - 8 : across] += change[8:16]
        return carry

    lax.fori_loop(0, planes, second_change, 0)

    sent("class", "slab", "near0", "far0", "near1", "far1", "edge")

    def leave(k, carry):
        block_copy(k).wait_send()
        return carry

    lax.fori_loop(1, count, leave, 0)


def shards(
    regional,
    row_weight,
    row_seg,
    row_col,
    box_owner,
    cell_class,
    soil_props,
    build_props,
    real_ids,
    disp_prev,
    disp_now,
):
    count = lax.axis_size("tile")
    planes, _, _, across, depth = disp_now.shape
    capacity = max(2, 2 * regional.shape[0] // count)
    cap = -(-capacity // 8) * 8
    block = 6 * cap + 8
    plane = (across, depth)
    f32 = jnp.float32
    vmem = pl.BlockSpec(memory_space=pltpu.VMEM)
    smem = pl.BlockSpec(memory_space=pltpu.SMEM)
    hbm = pl.BlockSpec(memory_space=pl.ANY)
    result = pl.pallas_call(
        functools.partial(body, count, cap),
        out_shape=jax.ShapeDtypeStruct((planes, 3) + plane, f32),
        in_specs=[vmem] * 4 + [smem] + [vmem] * 2 + [smem] + [hbm] * 3,
        out_specs=vmem,
        scratch_shapes=[
            pltpu.VMEM((planes + 2,) + plane, jnp.int32),
            pltpu.VMEM((planes + 6, 16, depth), jnp.int32),
            pltpu.VMEM((planes, 3) + plane, f32),
            pltpu.VMEM((planes + 4, 3) + plane, f32),
            pltpu.VMEM((planes + 4, 3) + plane, f32),
            pltpu.VMEM((planes + 2,) + plane, f32),
            pltpu.VMEM((planes + 2,) + plane, f32),
            pltpu.VMEM((planes,) + plane, f32),
            pltpu.VMEM((planes + 2,) + plane, f32),
            pltpu.VMEM((planes + 6, 3, 16, depth), f32),
            pltpu.VMEM((planes + 8, 3, 16, depth), f32),
            pltpu.VMEM((planes + 4, 3, 16, depth), f32),
            pltpu.VMEM((2, 6, 16, depth), f32),
            pltpu.VMEM((2, 6, 16, depth), f32),
            pltpu.VMEM((planes + 4, 3, 16, depth), f32),
            pltpu.VMEM((planes + 2, 16, depth), f32),
            pltpu.VMEM((count, block, depth), f32),
            pltpu.VMEM((count, block, depth), f32),
            pltpu.SemaphoreType.DMA((5,)),
            pltpu.SemaphoreType.DMA((count,)),
            pltpu.SemaphoreType.DMA((count,)),
            pltpu.SemaphoreType.DMA((14,)),
            pltpu.SemaphoreType.DMA((14,)),
        ],
        compiler_params=pltpu.CompilerParams(
            collective_id=0, has_side_effects=True, vmem_limit_bytes=56 * 1024 * 1024
        ),
        cost_estimate=pl.CostEstimate(
            flops=200 * planes * across * depth * 3,
            bytes_accessed=40 * planes * across * depth,
            transcendentals=0,
        ),
    )(
        regional,
        row_weight.reshape(1, -1),
        row_seg.reshape(1, -1),
        row_col.reshape(1, -1),
        box_owner[None],
        soil_props,
        jnp.transpose(build_props, (1, 0, 2)),
        real_ids,
        cell_class,
        disp_prev.reshape((planes, 3) + plane),
        disp_now.reshape((planes, 3) + plane),
    )
    return result.reshape(disp_now.shape)


def solution(mesh):
    row = P(("scen", "tile"), None)
    cell = P(("scen", "tile"), None, None)
    field = P(("scen", "tile"), None, None, None, None)
    return jax.shard_map(
        shards,
        mesh=mesh,
        in_specs=(row, row, row, row, P("scen"), cell, P(), P(), P("scen"), field, field),
        out_specs=field,
        check_vma=False,
    )
```
